768 devices in a mesh: grp: 96 (over x, z, core), own: 8 (over y).
Axes of the slice: x: 4, y: 8, z: 12, core: 2. Of those that a mesh axis runs over, the one named last changes fastest.
Arguments:
- lookup_slot: int32 [98304, 26], P(('grp', 'own')), may hold values from 0 to 5119, as said below
- emb_cot: bfloat16 [98304, 26, 128], P(('grp', 'own')), may hold values from -0.796875 to 0.796875
- slot_row: int32 [768, 1024], P(('grp', 'own')), may hold values from 0 to 2047, as said below
- slot_count: int32 [768, 8], P(('grp', 'own')), may hold values from 32 to 128, as said below
- bottom_act: bfloat16 [98304, 256], P(('grp', 'own')), may hold values from -6 to 6
- bottom_cot: bfloat16 [98304, 128], P(('grp', 'own')), may hold values from -0.039794922 to 0.039794922
Outputs:
- freq_grad: float32 [4096, 128], replicated
- table_grad: float32 [1572864, 128], P(('grp', 'own'))
- weight_grad: float32 [256, 128], replicated
- bias_grad: float32 [128], replicated
The draws below stay inside these ranges and needn't reach their ends.
Inputs may be any that keep to these rules, and one draw needn't show every extreme that they name: `slot_count`: each device sends its owners between 32 and 128 slots; in every group one owner, drawn from the seed, receives exactly 128 from every device of the group, and one device, drawn from the seed, sends exactly 128 to every owner. `slot_row`: within one device the live slots for one owner name distinct rows; slots past the device's total are 0 and no lookup names them. `lookup_slot`: every live slot of a device is named by one or more of its lookups; infrequent values stay below 4096 plus the device's total of slot_count.
All inputs are finite; a program needn't handle non-finite values.
Results may differ from the reference program's by a relative error of at most 0.0003.
Values sent between devices are 32-bit elements; how exact they have to be, the bound alone decides.
A program may use at most 32 MiB of HBM per device.

```python
import jax
import jax.numpy as jnp
from jax import lax

EMB = 128
F = 26
BOT_IN = 256
BOT_OUT = 128
SAMP_DEV = 128
FREQ = 4096
CAP = 128
ROWS_OWN = 2048
DEVS = 768
BATCH = 98304
N_GRP = 96
N_OWN = 8


def counts_for(key):
    key_base, key_hot, key_full = jax.random.split(jax.random.fold_in(key, 11), 3)
    base_counts = jax.random.randint(key_base, (DEVS, N_OWN), CAP // 4, CAP + 1)
    hot_owner = jax.random.randint(key_hot, (N_GRP,), 0, N_OWN)
    hot_device = jnp.repeat(hot_owner, N_OWN)
    is_hot = jnp.arange(N_OWN)[None, :] == hot_device[:, None]
    full_device = jax.random.randint(key_full, (), 0, DEVS)
    is_full = (jnp.arange(DEVS) == full_device)[:, None]
    return jnp.where(is_hot | is_full, CAP, base_counts).astype(jnp.int32)


def draw_slot_count(key, part):
    return counts_for(key)


def draw_slot_row(key, part):
    counts = counts_for(key)
    key = jax.random.fold_in(key, 3)
    scores = jax.random.randint(key, (DEVS, N_OWN, ROWS_OWN), 0, 4096) * ROWS_OWN + jnp.arange(ROWS_OWN)[None, None, :]
    chosen = jnp.argsort(scores, axis=2)[:, :, :CAP].astype(jnp.int32)
    slot_ends = jnp.cumsum(counts, axis=1)
    starts = slot_ends - counts
    positions = jnp.arange(N_OWN * CAP, dtype=jnp.int32)
    owner_of = jnp.sum((positions[None, :, None] >= slot_ends[:, None, :]).astype(jnp.int32), axis=2)
    safe_owner = jnp.minimum(owner_of, N_OWN - 1)
    first_slot = jnp.take_along_axis(starts, safe_owner, axis=1)
    within = jnp.clip(positions[None, :] - first_slot, 0, CAP - 1)
    flat_rows = chosen.reshape(DEVS, N_OWN * CAP)
    row_value = jnp.take_along_axis(flat_rows, safe_owner * CAP + within, axis=1)
    return jnp.where(positions[None, :] < slot_ends[:, -1:], row_value, 0).astype(jnp.int32)


def draw_lookup_slot(key, part):
    counts = counts_for(key)
    totals = jnp.sum(counts, axis=1)
    key = jax.random.fold_in(key, 5)
    key_order, key_extra, key_reuse, key_freq = jax.random.split(key, 4)
    lookups = SAMP_DEV * F
    scores = jax.random.randint(key_order, (DEVS, lookups), 0, 4096) * lookups + jnp.arange(lookups)[None, :]
    rank = jnp.argsort(jnp.argsort(scores, axis=1), axis=1).astype(jnp.int32)
    extra = jax.random.randint(key_extra, (DEVS, lookups), 0, 2) == 1
    reuse = jax.random.randint(key_reuse, (DEVS, lookups), 0, 1 << 20) % totals[:, None]
    first_use = rank < totals[:, None]
    slot_value = jnp.where(first_use, rank, reuse)
    infrequent = first_use | extra
    freq_id = jax.random.randint(key_freq, (DEVS, lookups), 0, FREQ)
    return jnp.where(infrequent, FREQ + slot_value, freq_id).reshape(BATCH, F).astype(jnp.int32)


def block_levels(rng, shape, cuts, least, largest):
    def one(position, blocks):
        steps = jax.random.uniform(jax.random.fold_in(jax.random.fold_in(rng, 6), position), (blocks,), jnp.float32, least / len(cuts), largest / len(cuts))
        return jnp.repeat(jnp.exp(steps), shape[position] // blocks).reshape((-1,) + (1,) * (len(shape) - position - 1))

    loudness = one(*cuts[0])
    for cut in cuts[1:]:
        loudness = loudness * one(*cut)
    return loudness


def bell_draw(own_key, shape, width, bound, cuts=(), kind=jnp.bfloat16):
    result = jax.random.normal(own_key, shape, jnp.float32) * width
    if len(cuts) > 0:
        result = block_levels(own_key, shape, cuts, -0.22, 0.18) * result
    return jnp.clip(result, min=-bound, max=bound).astype(kind)


def setup_inputs(seed: int = 0) -> dict:
    seeds = jax.random.split(jax.random.key(seed), 7)
    lookup_slot = draw_lookup_slot(jax.random.fold_in(seeds[6], 71), 0)
    emb_cot = bell_draw(seeds[1], (BATCH, F, EMB), 0.1, 0.796875, ((0, 768),))
    slot_row = draw_slot_row(jax.random.fold_in(seeds[6], 71), 0)
    slot_count = draw_slot_count(jax.random.fold_in(seeds[6], 71), 0)
    bottom_act = bell_draw(seeds[4], (BATCH, BOT_IN), 1.0, 6.0, ((0, 768),))
    bottom_cot = bell_draw(seeds[5], (BATCH, BOT_OUT), 0.005, 0.039794922, ((0, 768),))
    return dict(lookup_slot=lookup_slot, emb_cot=emb_cot, slot_row=slot_row, slot_count=slot_count, bottom_act=bottom_act, bottom_cot=bottom_cot)


def reference(lookup_slot, emb_cot, slot_row, slot_count, bottom_act, bottom_cot):
    lookups = SAMP_DEV * F
    group_ids = lookup_slot.reshape(N_GRP, N_OWN, lookups)
    group_cot = emb_cot.reshape(N_GRP, N_OWN * lookups, EMB)
    group_rows = slot_row.reshape(N_GRP, N_OWN, N_OWN * CAP)
    group_counts = slot_count.reshape(N_GRP, N_OWN, N_OWN)

    def one_group(pieces):
        lookup_ids, cot_rows, slot_rows, counts = pieces
        slot_ends = jnp.cumsum(counts, axis=1)
        packed = lookup_ids - FREQ
        owner_of = jnp.sum((packed[:, :, None] >= slot_ends[:, None, :]).astype(jnp.int32), axis=2)
        safe_slot = jnp.clip(packed, 0, N_OWN * CAP - 1).astype(jnp.int32)
        row_of = jnp.take_along_axis(slot_rows, safe_slot, axis=1)
        frequent = lookup_ids < FREQ
        dest_rows = jnp.where(frequent, N_OWN * ROWS_OWN, owner_of * ROWS_OWN + row_of).reshape(-1).astype(jnp.int32)
        freq_dest = jnp.where(frequent, lookup_ids, FREQ).reshape(-1).astype(jnp.int32)
        values = cot_rows.astype(jnp.float32)
        table_part = jax.ops.segment_sum(values, dest_rows, N_OWN * ROWS_OWN + 1)[:-1]
        freq_part = jax.ops.segment_sum(values, freq_dest, FREQ + 1)[:FREQ]
        return freq_part, table_part

    freq_parts, tables = lax.map(one_group, (group_ids, group_cot, group_rows, group_counts))
    freq_grad = jnp.sum(freq_parts, axis=0)
    table_grad = tables.reshape(N_GRP * N_OWN * ROWS_OWN, EMB)
    weight_grad = jnp.dot(bottom_act.T, bottom_cot, preferred_element_type=jnp.float32)
    bias_grad = jnp.sum(bottom_cot.astype(jnp.float32), axis=0)
    return freq_grad, table_grad, weight_grad, bias_grad
```

```python
import functools

import jax
import jax.numpy as jnp
from jax import lax
from jax.experimental import pallas as pl
from jax.experimental.pallas import tpu as pltpu
from jax.sharding import PartitionSpec as P

MESH = pl.DeviceIdType.MESH
F32 = jnp.float32
BF16 = jnp.bfloat16

NX, NY, NZ = 4, 8, 12
FREQ = 4096
EMB = 128
SLOTS = 1024
CAP = 128
ROWS_OWN = 2048
HALF = FREQ // 2
FX = HALF // NX
WX = 128 // NX
R1 = 576
R2 = R1 // NY
R3 = R2 // NZ
BLK = 256
VMEM_LIMIT = 40 * 2**20


def nearest_last(n):
    return sorted(range(1, n), key=lambda d: -min(d, n - d))


def onehot_bf16(rows_rel, iota_bf):
    return jnp.where(iota_bf == rows_rel, jnp.ones((), BF16), jnp.zeros((), BF16))


def relative(ids, base, size):
    rel = ids - base
    ok = (rel >= 0) & (rel < size)
    return jnp.where(ok, rel, -1).astype(F32).astype(BF16)


def main_kernel(
    ids_ref, emb_ref, slot_row_ref, counts_ref, act_ref, cot_ref,
    g_ref, table_ref,
    rhs, hi_s, part, rc, rx, s1, ry, s2z, rz, gz, t72, wsc, sg, ra, ssem, rsem,
):
    g = lax.axis_index("grp")
    y = lax.axis_index("own")
    x = g // (2 * NZ)
    z = (g // 2) % NZ
    c = g % 2

    def dev(xx, yy, zz, cc):
        return (xx * (2 * NZ) + zz * 2 + cc, yy)

    def to_x(d):
        return dev((x + d) % NX, y, z, c)

    def to_y(d):
        return dev(x, (y + d) % NY, z, c)

    def to_z(d):
        return dev(x, y, (z + d) % NZ, c)

    to_c = dev(x, y, z, 1 - c)

    used = [0]

    def copy(src, dst, target):
        i = used[0]
        used[0] += 1
        cp = pltpu.make_async_remote_copy(
            src_ref=src, dst_ref=dst, send_sem=ssem.at[i], recv_sem=rsem.at[i],
            device_id=target, device_id_type=MESH,
        )
        cp.start()
        return cp

    order_x, order_y, order_z = nearest_last(NX), nearest_last(NY), nearest_last(NZ)
    barrier = pltpu.get_barrier_semaphore()
    peers = [to_c] + [to_x(d) for d in order_x] + [to_y(d) for d in order_y] + [to_z(d) for d in order_z]
    for p in peers:
        pl.semaphore_signal(barrier, inc=1, device_id=p, device_id_type=MESH)

    counts = [counts_ref[0, p] for p in range(NY)]
    ends, total = [], 0
    for p in range(NY):
        total = total + counts[p]
        ends.append(total)
    starts = [e - n for e, n in zip(ends, counts)]
    ids = ids_ref[...]
    packed = ids - FREQ
    slot = packed
    for p in range(NY - 1):
        slot = slot + jnp.where(packed >= ends[p], CAP - counts[p], 0)
    freq = ids < FREQ
    hi_s[...] = jnp.where(freq, ids & (HALF - 1), HALF + (slot & (SLOTS // 2 - 1)))
    lo = jnp.where(freq, ids >> 11, slot >> 9).astype(F32)
    nf = ids.shape[0]
    for f in range(nf):
        col = jnp.transpose(jnp.broadcast_to(lo[f : f + 1, :], (128, 128)))
        v = emb_ref[f * 128 : (f + 1) * 128, :]
        right = v * col.astype(BF16)
        rhs[f * 128 : (f + 1) * 128, 0:128] = v * (1.0 - col).astype(BF16)
        rhs[f * 128 : (f + 1) * 128, 128:256] = right

    cot = cot_ref[...]
    wsc[...] = lax.dot_general(act_ref[...], cot, (((0,), (0,)), ((), ())), preferred_element_type=F32)
    bias = jnp.sum(cot.astype(F32), axis=0, keepdims=True)

    iota_bf = lax.broadcasted_iota(jnp.int32, (BLK, 128), 0).astype(F32).astype(BF16)

    def block_sum(base):
        rel = relative(hi_s[...], base, BLK)
        lhs = jnp.concatenate([onehot_bf16(rel[f : f + 1, :], iota_bf) for f in range(nf)], axis=1)
        return jnp.dot(lhs, rhs[...], preferred_element_type=F32)

    order = order_x + [0]
    c_copies = []
    x_copies = []

    def after_core(k):
        o = order[k]
        c_copies[k].wait()
        rc[o] = rc[o] + part[c, o]
        if o != 0:
            x_copies.append(copy(rc.at[o], rx.at[o - 1], to_x(o)))

    for k, o in enumerate(order):
        px = (x + o) % NX

        @pl.loop(0, FX // BLK)
        def _(b, o=o, px=px):
            acc = block_sum(px * FX + b * BLK)
            at = pl.ds(pl.multiple_of(b * BLK, BLK), BLK)
            part[0, o, at, :] = acc[:, 0:128]
            part[1, o, at, :] = acc[:, 128:256]

        for h in range(2):
            part[h, o, FX : FX + WX, :] = wsc[pl.ds(pl.multiple_of(h * 128 + px * WX, WX), WX), :]
            part[h, o, FX + WX : FX + WX + 8, :] = jnp.broadcast_to(bias, (8, 128))
            part[h, o, FX + WX + 8 : R1, :] = jnp.zeros((R1 - FX - WX - 8, 128), F32)
        if k == 0:
            pl.semaphore_wait(barrier, len(peers))
        c_copies.append(copy(part.at[1 - c, o], rc.at[o], to_c))
        if k > 0:
            after_core(k - 1)
    after_core(len(order) - 1)

    @pl.loop(0, SLOTS // 2 // BLK)
    def _(b):
        acc = block_sum(HALF + b * BLK)
        for q in range(BLK // CAP):
            sg[b * (BLK // CAP) + q, 0:CAP, :] = acc[q * CAP : (q + 1) * CAP, 0:128]
            sg[NY // 2 + b * (BLK // CAP) + q, 0:CAP, :] = acc[q * CAP : (q + 1) * CAP, 128:256]

    for cp in x_copies:
        cp.wait()
    s1[...] = (rc[0] + rx[0]) + (rx[1] + rx[2])

    def rows_y(k):
        return pl.ds(pl.multiple_of(k * R2, 8), R2)

    y_copies = [copy(s1.at[rows_y((y + d) % NY)], ry.at[d - 1], to_y(d)) for d in order_y]

    sr = jnp.broadcast_to(slot_row_ref[...], (8, SLOTS))
    which = lax.broadcasted_iota(jnp.int32, (8, SLOTS), 0)
    parts = jnp.where(which == 0, sr >> 4, sr & 15).astype(F32).astype(BF16)
    diff = lax.broadcasted_iota(jnp.int32, (SLOTS, CAP), 0) - lax.broadcasted_iota(jnp.int32, (SLOTS, CAP), 1)
    lane = lax.broadcasted_iota(jnp.int32, (8, CAP), 1)
    for p in range(NY):
        pick = jnp.where(diff == starts[p], 1.0, 0.0).astype(BF16)
        both = jnp.dot(parts, pick, preferred_element_type=F32)
        row = both[0:1, :] * 16.0 + both[1:2, :]
        row = jnp.where(lane < counts[p], jnp.broadcast_to(row, (8, CAP)), 0.0)
        sg[p, CAP : CAP + 8, :] = row

    for cp in y_copies:
        cp.wait()
    s2 = s1[rows_y(y), :]
    for d in range(1, NY):
        s2 = s2 + ry[d - 1]
    for k in range(NZ):
        s2z[k] = s2[k * R3 : (k + 1) * R3, :]

    z_copies = [copy(s2z.at[(z + d) % NZ], rz.at[d - 1], to_z(d)) for d in order_z]
    a_copies = [copy(sg.at[(y + d) % NY], ra.at[d], to_y(d)) for d in order_y]
    ra[0] = sg[y]
    for cp in z_copies:
        cp.wait()
    s3 = s2z[z]
    for d in range(1, NZ):
        s3 = s3 + rz[d - 1]
    gz[z] = s3
    zg_copies = [copy(gz.at[z], gz.at[z], to_z(d)) for d in order_z]

    for cp in a_copies:
        cp.wait()
    for d in range(NY):
        v = ra[d, 0:CAP, :]
        top = v.astype(BF16)
        rhs[d * CAP : (d + 1) * CAP, 0:128] = top
        rhs[d * CAP : (d + 1) * CAP, 128:256] = (v - top.astype(F32)).astype(BF16)

    @pl.loop(0, ROWS_OWN // BLK)
    def _(b):
        cols = []
        for d in range(NY):
            rel = relative(ra[d, CAP : CAP + 8, :].astype(jnp.int32), b * BLK, BLK)
            cols.append(onehot_bf16(rel[0:1, :], iota_bf))
        lhs = jnp.concatenate(cols, axis=1)
        acc = jnp.dot(lhs, rhs[0:SLOTS, :], preferred_element_type=F32)
        table_ref[pl.ds(pl.multiple_of(b * BLK, BLK), BLK), :] = acc[:, 0:128] + acc[:, 128:256]

    for cp in zg_copies:
        cp.wait()
    for k in range(NZ):
        t72[k * R3 : (k + 1) * R3, :] = gz[k]

    g_ref[c, x, rows_y(y), :] = t72[...]
    yg_copies = [copy(t72, g_ref.at[c, x, rows_y(y)], to_y(d)) for d in order_y]
    for cp in yg_copies:
        cp.wait()
    xg_copies = [copy(g_ref.at[c, x], g_ref.at[c, x], to_x(d)) for d in order_x]
    cg_copies = [copy(g_ref.at[c, x], g_ref.at[c, x], to_c)]
    for d, cp in zip(order_x, xg_copies):
        cp.wait_recv()
        xs = (x - d + NX) % NX
        cg_copies.append(copy(g_ref.at[c, xs], g_ref.at[c, xs], to_c))
    for cp in xg_copies:
        cp.wait_send()
    for cp in cg_copies:
        cp.wait()


N_COPIES = NX + (NX - 1) + 3 * (NY - 1) + 2 * (NZ - 1) + (NX - 1) + NX


def finish_kernel(g_ref, table_in, freq_ref, table_ref, weight_ref, bias_ref, sem):
    cps = []

    def copy(src, dst):
        cp = pltpu.make_async_copy(src, dst, sem.at[len(cps)])
        cp.start()
        cps.append(cp)

    for h in range(2):
        for k in range(NX):
            copy(g_ref.at[h, k, 0:FX], freq_ref.at[pl.ds(h * HALF + k * FX, FX)])
            copy(g_ref.at[h, k, FX : FX + WX], weight_ref.at[pl.ds(h * 128 + k * WX, WX)])
    copy(table_in, table_ref)
    bias_ref[...] = g_ref[0, 0, FX + WX : FX + WX + 1, :]
    for cp in cps:
        cp.wait()


def per_device(lookup_slot, emb_cot, slot_row, slot_count, bottom_act, bottom_cot):
    n, f = lookup_slot.shape
    ids = lookup_slot.T
    emb = jnp.transpose(emb_cot, (1, 0, 2)).reshape(f * n, EMB)
    vm = pl.BlockSpec(memory_space=pltpu.VMEM)
    sm = pl.BlockSpec(memory_space=pltpu.SMEM)
    anym = pl.BlockSpec(memory_space=pl.ANY)
    gathered, table = pl.pallas_call(
        main_kernel,
        out_shape=(pltpu.VMEM((2, NX, R1, 128), F32), pltpu.VMEM((ROWS_OWN, 128), F32)),
        in_specs=[vm, vm, vm, sm, vm, vm],
        out_specs=(vm, vm),
        scratch_shapes=[
            pltpu.VMEM((f * n, 256), BF16),
            pltpu.VMEM((f, n), jnp.int32),
            pltpu.VMEM((2, NX, R1, 128), F32),
            pltpu.VMEM((NX, R1, 128), F32),
            pltpu.VMEM((NX - 1, R1, 128), F32),
            pltpu.VMEM((R1, 128), F32),
            pltpu.VMEM((NY - 1, R2, 128), F32),
            pltpu.VMEM((NZ, R3, 128), F32),
            pltpu.VMEM((NZ - 1, R3, 128), F32),
            pltpu.VMEM((NZ, R3, 128), F32),
            pltpu.VMEM((R2, 128), F32),
            pltpu.VMEM((256, 128), F32),
            pltpu.VMEM((NY, CAP + 8, 128), F32),
            pltpu.VMEM((NY, CAP + 8, 128), F32),
            pltpu.SemaphoreType.DMA((N_COPIES,)),
            pltpu.SemaphoreType.DMA((N_COPIES,)),
        ],
        compiler_params=pltpu.CompilerParams(
            collective_id=0, has_side_effects=True, vmem_limit_bytes=VMEM_LIMIT
        ),
    )(ids, emb, slot_row, slot_count, bottom_act, bottom_cot)
    freq_grad, table_grad, weight_grad, bias_row = pl.pallas_call(
        finish_kernel,
        out_shape=(
            jax.ShapeDtypeStruct((FREQ, 128), F32),
            jax.ShapeDtypeStruct((ROWS_OWN, 128), F32),
            jax.ShapeDtypeStruct((256, 128), F32),
            jax.ShapeDtypeStruct((1, 128), F32),
        ),
        in_specs=[vm, vm],
        out_specs=(anym, anym, anym, vm),
        scratch_shapes=[pltpu.SemaphoreType.DMA((4 * NX + 1,))],
        compiler_params=pltpu.CompilerParams(vmem_limit_bytes=4 * 2**20),
    )(
        pltpu.with_memory_space_constraint(gathered, pltpu.VMEM),
        pltpu.with_memory_space_constraint(table, pltpu.VMEM),
    )
    return freq_grad, table_grad, weight_grad, bias_row.reshape(128)


def solution(mesh):
    placed = (
        P(("grp", "own"), None),
        P(("grp", "own"), None, None),
        P(("grp", "own"), None),
        P(("grp", "own"), None),
        P(("grp", "own"), None),
        P(("grp", "own"), None),
    )
    return jax.shard_map(
        per_device,
        mesh=mesh,
        in_specs=placed,
        out_specs=(P(), P(("grp", "own"), None), P(), P()),
        check_vma=False,
    )
```

```python
import functools

import jax
import jax.numpy as jnp
from jax import lax
from jax.experimental import pallas as pl
from jax.experimental.pallas import tpu as pltpu
from jax.sharding import PartitionSpec as P

MESH = pl.DeviceIdType.MESH
F32 = jnp.float32
BF16 = jnp.bfloat16

NX, NY, NZ = 4, 8, 12
FREQ = 4096
EMB = 128
SLOTS = 1024
CAP = 128
ROWS_OWN = 2048
HALF = FREQ // 2
FX = HALF // NX
WX = 128 // NX
R1 = 576
R2 = R1 // NY
R3 = R2 // NZ
BLK = 256
VMEM_LIMIT = 40 * 2**20


def nearest_last(n):
    return sorted(range(1, n), key=lambda d: -min(d, n - d))


def onehot_bf16(rows_rel, iota_bf):
    return jnp.where(iota_bf == rows_rel, jnp.ones((), BF16), jnp.zeros((), BF16))


def relative(ids, base, size):
    rel = ids - base
    ok = (rel >= 0) & (rel < size)
    return jnp.where(ok, rel, -1).astype(F32).astype(BF16)


def main_kernel(
    ids_in, emb_in, slot_row_in, counts_in, act_in, cot_in,
    g_ref, table_ref,
    ids_ref, emb_ref, slot_row_ref, counts_ref, act_ref, cot_ref, isem,
    rhs, hi_s, part, rc, rx, s1, ry, s2z, rz, gz, t72, wsc, sg, ra, ssem, rsem,
):
    loads = [
        pltpu.make_async_copy(src, dst, isem.at[i])
        for i, (src, dst) in enumerate((
            (counts_in, counts_ref), (ids_in, ids_ref), (emb_in, emb_ref),
            (cot_in, cot_ref), (act_in, act_ref), (slot_row_in, slot_row_ref),
        ))
    ]
    for ld in loads:
        ld.start()

    g = lax.axis_index("grp")
    y = lax.axis_index("own")
    x = g // (2 * NZ)
    z = (g // 2) % NZ
    c = g % 2

    def dev(xx, yy, zz, cc):
        return (xx * (2 * NZ) + zz * 2 + cc, yy)

    def to_x(d):
        return dev((x + d) % NX, y, z, c)

    def to_y(d):
        return dev(x, (y + d) % NY, z, c)

    def to_z(d):
        return dev(x, y, (z + d) % NZ, c)

    to_c = dev(x, y, z, 1 - c)

    used = [0]
    sends = []

    def copy(src, dst, target):
        i = used[0]
        used[0] += 1
        cp = pltpu.make_async_remote_copy(
            src_ref=src, dst_ref=dst, send_sem=ssem.at[i], recv_sem=rsem.at[i],
            device_id=target, device_id_type=MESH,
        )
        cp.start()
        sends.append(cp)
        return cp

    order_x, order_y, order_z = [2, 1, 3], nearest_last(NY), nearest_last(NZ)
    barrier = pltpu.get_barrier_semaphore()
    peers = [to_c] + [to_x(d) for d in (1, 3)] + [to_y(d) for d in order_y] + [to_z(d) for d in order_z]
    for p in peers:
        pl.semaphore_signal(barrier, inc=1, device_id=p, device_id_type=MESH)

    for ld in loads:
        ld.wait()

    counts = [counts_ref[0, p] for p in range(NY)]
    ends, total = [], 0
    for p in range(NY):
        total = total + counts[p]
        ends.append(total)
    starts = [e - n for e, n in zip(ends, counts)]
    ids = ids_ref[...]
    packed = ids - FREQ
    slot = packed
    for p in range(NY - 1):
        slot = slot + jnp.where(packed >= ends[p], CAP - counts[p], 0)
    freq = ids < FREQ
    hi_s[...] = jnp.where(freq, ids & (HALF - 1), HALF + (slot & (SLOTS // 2 - 1)))
    lo = jnp.where(freq, ids >> 11, slot >> 9).astype(F32)
    nf = ids.shape[0]
    for f in range(nf):
        col = jnp.transpose(jnp.broadcast_to(lo[f : f + 1, :], (128, 128)))
        v = emb_ref[f * 128 : (f + 1) * 128, :]
        right = v * col.astype(BF16)
        rhs[f * 128 : (f + 1) * 128, 0:128] = v * (1.0 - col).astype(BF16)
        rhs[f * 128 : (f + 1) * 128, 128:256] = right

    cot = cot_ref[...]
    wsc[...] = lax.dot_general(act_ref[...], cot, (((0,), (0,)), ((), ())), preferred_element_type=F32)
    bias = jnp.sum(cot.astype(F32), axis=0, keepdims=True)

    iota_bf = lax.broadcasted_iota(jnp.int32, (BLK, 128), 0).astype(F32).astype(BF16)

    def block_sum(base):
        rel = relative(hi_s[...], base, BLK)
        lhs = jnp.concatenate([onehot_bf16(rel[f : f + 1, :], iota_bf) for f in range(nf)], axis=1)
        return jnp.dot(lhs, rhs[...], preferred_element_type=F32)

    order = order_x + [0]
    c_copies = []
    x_copies = {}
    half_a, half_b = pl.ds(0, R1 // 2), pl.ds(R1 // 2, R1 // 2)

    def after_core(k):
        o = order[k]
        c_copies[k].wait_recv()
        rc[o] = rc[o] + part[c, o]
        if o == 2:
            x_copies[0] = copy(rc.at[2, half_a], rx.at[0], to_x(1))
            x_copies[1] = copy(rc.at[2, half_b], rx.at[1], to_x(3))
        if o == 1:
            x_copies[2] = copy(rc.at[1, half_b], rx.at[2], to_x(1))
        if o == 3:
            x_copies[3] = copy(rc.at[3, half_a], rx.at[3], to_x(3))

    for k, o in enumerate(order):
        px = (x + o) % NX

        @pl.loop(0, FX // BLK)
        def _(b, o=o, px=px):
            acc = block_sum(px * FX + b * BLK)
            at = pl.ds(pl.multiple_of(b * BLK, BLK), BLK)
            part[0, o, at, :] = acc[:, 0:128]
            part[1, o, at, :] = acc[:, 128:256]

        for h in range(2):
            part[h, o, FX : FX + WX, :] = wsc[pl.ds(pl.multiple_of(h * 128 + px * WX, WX), WX), :]
            part[h, o, FX + WX : FX + WX + 8, :] = jnp.broadcast_to(bias, (8, 128))
            part[h, o, FX + WX + 8 : R1, :] = jnp.zeros((R1 - FX - WX - 8, 128), F32)
        if k == 0:
            pl.semaphore_wait(barrier, len(peers))
        c_copies.append(copy(part.at[1 - c, o], rc.at[o], to_c))
        if k > 0:
            after_core(k - 1)
    after_core(len(order) - 1)

    @pl.loop(0, SLOTS // 2 // BLK)
    def _(b):
        acc = block_sum(HALF + b * BLK)
        for q in range(BLK // CAP):
            sg[b * (BLK // CAP) + q, 0:CAP, :] = acc[q * CAP : (q + 1) * CAP, 0:128]
            sg[NY // 2 + b * (BLK // CAP) + q, 0:CAP, :] = acc[q * CAP : (q + 1) * CAP, 128:256]

    x_copies[0].wait_recv()
    rc[1, half_a, :] = rc[1, half_a, :] + rx[0]
    x_copies[4] = copy(rc.at[1, half_a], rx.at[4], to_x(1))
    x_copies[1].wait_recv()
    rc[3, half_b, :] = rc[3, half_b, :] + rx[1]
    x_copies[5] = copy(rc.at[3, half_b], rx.at[5], to_x(3))

    sr = jnp.broadcast_to(slot_row_ref[...], (8, SLOTS))
    which = lax.broadcasted_iota(jnp.int32, (8, SLOTS), 0)
    parts = jnp.where(which == 0, sr >> 4, sr & 15).astype(F32).astype(BF16)
    diff = lax.broadcasted_iota(jnp.int32, (SLOTS, CAP), 0) - lax.broadcasted_iota(jnp.int32, (SLOTS, CAP), 1)
    lane = lax.broadcasted_iota(jnp.int32, (8, CAP), 1)
    for p in range(NY):
        pick = jnp.where(diff == starts[p], 1.0, 0.0).astype(BF16)
        both = jnp.dot(parts, pick, preferred_element_type=F32)
        row = both[0:1, :] * 16.0 + both[1:2, :]
        row = jnp.where(lane < counts[p], jnp.broadcast_to(row, (8, CAP)), 0.0)
        sg[p, CAP : CAP + 8, :] = row

    for i in range(2, 6):
        x_copies[i].wait_recv()
    s1[half_a, :] = rc[0, half_a, :] + (rx[3] + rx[4])
    s1[half_b, :] = rc[0, half_b, :] + (rx[2] + rx[5])

    def rows_y(k):
        return pl.ds(pl.multiple_of(k * R2, 8), R2)

    y_copies = [copy(s1.at[rows_y((y + d) % NY)], ry.at[d - 1], to_y(d)) for d in order_y]

    for cp in y_copies:
        cp.wait_recv()
    s2 = s1[rows_y(y), :]
    for d in range(1, NY):
        s2 = s2 + ry[d - 1]
    for k in range(NZ):
        s2z[k] = s2[k * R3 : (k + 1) * R3, :]

    z_copies = [copy(s2z.at[(z + d) % NZ], rz.at[d - 1], to_z(d)) for d in order_z]
    a_copies = [copy(sg.at[(y + d) % NY], ra.at[d], to_y(d)) for d in order_y]
    ra[0] = sg[y]
    for cp in z_copies:
        cp.wait_recv()
    s3 = s2z[z]
    for d in range(1, NZ):
        s3 = s3 + rz[d - 1]
    gz[z] = s3
    zg_copies = [copy(gz.at[z], gz.at[z], to_z(d)) for d in order_z]

    for cp in zg_copies:
        cp.wait_recv()
    for k in range(NZ):
        t72[k * R3 : (k + 1) * R3, :] = gz[k]

    g_ref[c, x, rows_y(y), :] = t72[...]
    yg_copies = [copy(t72, g_ref.at[c, x, rows_y(y)], to_y(d)) for d in order_y]

    for cp in a_copies:
        cp.wait_recv()
    for d in range(NY):
        v = ra[d, 0:CAP, :]
        top = v.astype(BF16)
        rhs[d * CAP : (d + 1) * CAP, 0:128] = top
        rhs[d * CAP : (d + 1) * CAP, 128:256] = (v - top.astype(F32)).astype(BF16)

    @pl.loop(0, ROWS_OWN // BLK)
    def _(b):
        cols = []
        for d in range(NY):
            rel = relative(ra[d, CAP : CAP + 8, :].astype(jnp.int32), b * BLK, BLK)
            cols.append(onehot_bf16(rel[0:1, :], iota_bf))
        lhs = jnp.concatenate(cols, axis=1)
        acc = jnp.dot(lhs, rhs[0:SLOTS, :], preferred_element_type=F32)
        table_ref[pl.ds(pl.multiple_of(b * BLK, BLK), BLK), :] = acc[:, 0:128] + acc[:, 128:256]

    for cp in yg_copies:
        cp.wait_recv()

    def pass_on(xs, rows, target):
        return copy(g_ref.at[c, xs, rows], g_ref.at[c, xs, rows], target)

    before, after, far = (x + NX - 1) % NX, (x + 1) % NX, (x + 2) % NX
    up_a = pass_on(x, half_a, to_x(1))
    down_b = pass_on(x, half_b, to_x(3))
    up_b = pass_on(x, half_b, to_x(1))
    down_a = pass_on(x, half_a, to_x(3))
    cg_copies = [copy(g_ref.at[c, x], g_ref.at[c, x], to_c)]
    up_a.wait_recv()
    far_a = pass_on(before, half_a, to_x(1))
    down_b.wait_recv()
    far_b = pass_on(after, half_b, to_x(3))
    cg_copies.append(pass_on(before, half_a, to_c))
    cg_copies.append(pass_on(after, half_b, to_c))
    for cp, xs, rows in ((up_b, before, half_b), (down_a, after, half_a), (far_a, far, half_a), (far_b, far, half_b)):
        cp.wait_recv()
        cg_copies.append(pass_on(xs, rows, to_c))
    for cp in cg_copies:
        cp.wait_recv()
    for cp in sends:
        cp.wait_send()


N_COPIES = NX + 6 + 3 * (NY - 1) + 2 * (NZ - 1) + 6 + 7


def finish_kernel(g_ref, table_in, freq_ref, table_ref, weight_ref, bias_ref, sem):
    cps = []

    def copy(src, dst):
        cp = pltpu.make_async_copy(src, dst, sem.at[len(cps)])
        cp.start()
        cps.append(cp)

    for h in range(2):
        for k in range(NX):
            copy(g_ref.at[h, k, 0:FX], freq_ref.at[pl.ds(h * HALF + k * FX, FX)])
            copy(g_ref.at[h, k, FX : FX + WX], weight_ref.at[pl.ds(h * 128 + k * WX, WX)])
    copy(table_in, table_ref)
    bias_ref[...] = g_ref[0, 0, FX + WX : FX + WX + 1, :]
    for cp in cps:
        cp.wait()


def per_device(lookup_slot, emb_cot, slot_row, slot_count, bottom_act, bottom_cot):
    n, f = lookup_slot.shape
    ids = lookup_slot.T
    emb = jnp.transpose(emb_cot, (1, 0, 2)).reshape(f * n, EMB)
    vm = pl.BlockSpec(memory_space=pltpu.VMEM)
    hbm = pl.BlockSpec(memory_space=pltpu.HBM)
    anym = pl.BlockSpec(memory_space=pl.ANY)
    gathered, table = pl.pallas_call(
        main_kernel,
        out_shape=(pltpu.VMEM((2, NX, R1, 128), F32), pltpu.VMEM((ROWS_OWN, 128), F32)),
        in_specs=[hbm] * 6,
        out_specs=(vm, vm),
        scratch_shapes=[
            pltpu.VMEM((f, n), jnp.int32),
            pltpu.VMEM((f * n, EMB), BF16),
            pltpu.VMEM(slot_row.shape, jnp.int32),
            pltpu.SMEM(slot_count.shape, jnp.int32),
            pltpu.VMEM(bottom_act.shape, BF16),
            pltpu.VMEM(bottom_cot.shape, BF16),
            pltpu.SemaphoreType.DMA((6,)),
            pltpu.VMEM((f * n, 256), BF16),
            pltpu.VMEM((f, n), jnp.int32),
            pltpu.VMEM((2, NX, R1, 128), F32),
            pltpu.VMEM((NX, R1, 128), F32),
            pltpu.VMEM((6, R1 // 2, 128), F32),
            pltpu.VMEM((R1, 128), F32),
            pltpu.VMEM((NY - 1, R2, 128), F32),
            pltpu.VMEM((NZ, R3, 128), F32),
            pltpu.VMEM((NZ - 1, R3, 128), F32),
            pltpu.VMEM((NZ, R3, 128), F32),
            pltpu.VMEM((R2, 128), F32),
            pltpu.VMEM((256, 128), F32),
            pltpu.VMEM((NY, CAP + 8, 128), F32),
            pltpu.VMEM((NY, CAP + 8, 128), F32),
            pltpu.SemaphoreType.DMA((N_COPIES,)),
            pltpu.SemaphoreType.DMA((N_COPIES,)),
        ],
        compiler_params=pltpu.CompilerParams(
            collective_id=0, has_side_effects=True, vmem_limit_bytes=VMEM_LIMIT
        ),
    )(*(pltpu.with_memory_space_constraint(a, pltpu.HBM) for a in (ids, emb, slot_row, slot_count, bottom_act, bottom_cot)))
    freq_grad, table_grad, weight_grad, bias_row = pl.pallas_call(
        finish_kernel,
        out_shape=(
            jax.ShapeDtypeStruct((FREQ, 128), F32),
            jax.ShapeDtypeStruct((ROWS_OWN, 128), F32),
            jax.ShapeDtypeStruct((256, 128), F32),
            jax.ShapeDtypeStruct((1, 128), F32),
        ),
        in_specs=[vm, vm],
        out_specs=(anym, anym, anym, vm),
        scratch_shapes=[pltpu.SemaphoreType.DMA((4 * NX + 1,))],
        compiler_params=pltpu.CompilerParams(vmem_limit_bytes=4 * 2**20),
    )(
        pltpu.with_memory_space_constraint(gathered, pltpu.VMEM),
        pltpu.with_memory_space_constraint(table, pltpu.VMEM),
    )
    return freq_grad, table_grad, weight_grad, bias_row.reshape(128)


def solution(mesh):
    placed = (
        P(("grp", "own"), None),
        P(("grp", "own"), None, None),
        P(("grp", "own"), None),
        P(("grp", "own"), None),
        P(("grp", "own"), None),
        P(("grp", "own"), None),
    )
    return jax.shard_map(
        per_device,
        mesh=mesh,
        in_specs=placed,
        out_specs=(P(), P(("grp", "own"), None), P(), P()),
        check_vma=False,
    )
```

```python
import functools

import jax
import jax.numpy as jnp
from jax import lax
from jax.experimental import pallas as pl
from jax.experimental.pallas import tpu as pltpu
from jax.sharding import PartitionSpec as P

MESH = pl.DeviceIdType.MESH
F32 = jnp.float32
BF16 = jnp.bfloat16

NX, NY, NZ = 4, 8, 12
FREQ = 4096
EMB = 128
SLOTS = 1024
CAP = 128
ROWS_OWN = 2048
HALF = FREQ // 2
FX = HALF // NX
WX = 128 // NX
R1 = 576
R2 = R1 // NY
R3 = R2 // NZ
BLK = 256
VMEM_LIMIT = 40 * 2**20


def nearest_last(n):
    return sorted(range(1, n), key=lambda d: -min(d, n - d))


def onehot_bf16(rows_rel, iota_bf):
    return jnp.where(iota_bf == rows_rel, jnp.ones((), BF16), jnp.zeros((), BF16))


def relative(ids, base, size):
    rel = ids - base
    ok = (rel >= 0) & (rel < size)
    return jnp.where(ok, rel, -1).astype(F32).astype(BF16)


def main_kernel(
    ids_in, emb_in, slot_row_in, counts_in, act_in, cot_in,
    g_ref, table_ref,
    ids_ref, emb_ref, slot_row_ref, counts_ref, act_ref, cot_ref, isem,
    rhs, hi_s, part, rc, rx, s1, ry, s2z, rz, gz, t72, wsc, sg, ra, ssem, rsem,
):
    loads = [
        pltpu.make_async_copy(src, dst, isem.at[i])
        for i, (src, dst) in enumerate((
            (counts_in, counts_ref), (ids_in, ids_ref), (emb_in, emb_ref),
            (cot_in, cot_ref), (act_in, act_ref), (slot_row_in, slot_row_ref),
        ))
    ]
    for ld in loads:
        ld.start()

    g = lax.axis_index("grp")
    y = lax.axis_index("own")
    x = g // (2 * NZ)
    z = (g // 2) % NZ
    c = g % 2

    def dev(xx, yy, zz, cc):
        return (xx * (2 * NZ) + zz * 2 + cc, yy)

    def to_x(d):
        return dev((x + d) % NX, y, z, c)

    def to_y(d):
        return dev(x, (y + d) % NY, z, c)

    def to_z(d):
        return dev(x, y, (z + d) % NZ, c)

    to_c = dev(x, y, z, 1 - c)

    used = [0]
    sends = []

    def copy(src, dst, target):
        i = used[0]
        used[0] += 1
        cp = pltpu.make_async_remote_copy(
            src_ref=src, dst_ref=dst, send_sem=ssem.at[i], recv_sem=rsem.at[i],
            device_id=target, device_id_type=MESH,
        )
        cp.start()
        sends.append(cp)
        return cp

    order_x, order_y, order_z = [2, 1, 3], nearest_last(NY), nearest_last(NZ)
    barrier = pltpu.get_barrier_semaphore()
    peers = [to_c] + [to_x(d) for d in (1, 3)] + [to_y(d) for d in order_y] + [to_z(d) for d in order_z]
    for p in peers:
        pl.semaphore_signal(barrier, inc=1, device_id=p, device_id_type=MESH)

    for ld in loads:
        ld.wait()

    counts = [counts_ref[0, p] for p in range(NY)]
    ends, total = [], 0
    for p in range(NY):
        total = total + counts[p]
        ends.append(total)
    starts = [e - n for e, n in zip(ends, counts)]
    ids = ids_ref[...]
    packed = ids - FREQ
    slot = packed
    for p in range(NY - 1):
        slot = slot + jnp.where(packed >= ends[p], CAP - counts[p], 0)
    freq = ids < FREQ
    hi_s[...] = jnp.where(freq, ids & (HALF - 1), HALF + (slot & (SLOTS // 2 - 1)))
    lo = jnp.where(freq, ids >> 11, slot >> 9).astype(F32)
    nf = ids.shape[0]
    for f in range(nf):
        col = jnp.transpose(jnp.broadcast_to(lo[f : f + 1, :], (128, 128)))
        v = emb_ref[f * 128 : (f + 1) * 128, :]
        right = v * col.astype(BF16)
        rhs[f * 128 : (f + 1) * 128, 0:128] = v * (1.0 - col).astype(BF16)
        rhs[f * 128 : (f + 1) * 128, 128:256] = right

    cot = cot_ref[...]
    wsc[...] = lax.dot_general(act_ref[...], cot, (((0,), (0,)), ((), ())), preferred_element_type=F32)
    bias = jnp.sum(cot.astype(F32), axis=0, keepdims=True)

    iota_bf = lax.broadcasted_iota(jnp.int32, (BLK, 128), 0).astype(F32).astype(BF16)

    def block_sum(base):
        rel = relative(hi_s[...], base, BLK)
        lhs = jnp.concatenate([onehot_bf16(rel[f : f + 1, :], iota_bf) for f in range(nf)], axis=1)
        return jnp.dot(lhs, rhs[...], preferred_element_type=F32)

    order = order_x + [0]
    c_copies = []
    x_copies = {}
    half_a, half_b = pl.ds(0, R1 // 2), pl.ds(R1 // 2, R1 // 2)

    def after_core(k):
        o = order[k]
        c_copies[k].wait_recv()
        rc[o] = rc[o] + part[c, o]
        if o == 2:
            x_copies[0] = copy(rc.at[2, half_a], rx.at[0], to_x(1))
            x_copies[1] = copy(rc.at[2, half_b], rx.at[1], to_x(3))
        if o == 1:
            x_copies[2] = copy(rc.at[1, half_b], rx.at[2], to_x(1))
        if o == 3:
            x_copies[3] = copy(rc.at[3, half_a], rx.at[3], to_x(3))

    for k, o in enumerate(order):
        px = (x + o) % NX

        @pl.loop(0, FX // BLK)
        def _(b, o=o, px=px):
            acc = block_sum(px * FX + b * BLK)
            at = pl.ds(pl.multiple_of(b * BLK, BLK), BLK)
            part[0, o, at, :] = acc[:, 0:128]
            part[1, o, at, :] = acc[:, 128:256]

        for h in range(2):
            part[h, o, FX : FX + WX, :] = wsc[pl.ds(pl.multiple_of(h * 128 + px * WX, WX), WX), :]
            part[h, o, FX + WX : FX + WX + 8, :] = jnp.broadcast_to(bias, (8, 128))
            part[h, o, FX + WX + 8 : R1, :] = jnp.zeros((R1 - FX - WX - 8, 128), F32)
        if k == 0:
            pl.semaphore_wait(barrier, len(peers))
        c_copies.append(copy(part.at[1 - c, o], rc.at[o], to_c))
        if k > 0:
            after_core(k - 1)
    after_core(len(order) - 1)

    @pl.loop(0, SLOTS // 2 // BLK)
    def _(b):
        acc = block_sum(HALF + b * BLK)
        for q in range(BLK // CAP):
            sg[b * (BLK // CAP) + q, 0:CAP, :] = acc[q * CAP : (q + 1) * CAP, 0:128]
            sg[NY // 2 + b * (BLK // CAP) + q, 0:CAP, :] = acc[q * CAP : (q + 1) * CAP, 128:256]

    x_copies[0].wait_recv()
    rc[1, half_a, :] = rc[1, half_a, :] + rx[0]
    x_copies[4] = copy(rc.at[1, half_a], rx.at[4], to_x(1))
    x_copies[1].wait_recv()
    rc[3, half_b, :] = rc[3, half_b, :] + rx[1]
    x_copies[5] = copy(rc.at[3, half_b], rx.at[5], to_x(3))

    sr = jnp.broadcast_to(slot_row_ref[...], (8, SLOTS))
    which = lax.broadcasted_iota(jnp.int32, (8, SLOTS), 0)
    parts = jnp.where(which == 0, sr >> 4, sr & 15).astype(F32).astype(BF16)
    diff = lax.broadcasted_iota(jnp.int32, (SLOTS, CAP), 0) - lax.broadcasted_iota(jnp.int32, (SLOTS, CAP), 1)
    lane = lax.broadcasted_iota(jnp.int32, (8, CAP), 1)
    for p in range(NY):
        pick = jnp.where(diff == starts[p], 1.0, 0.0).astype(BF16)
        both = jnp.dot(parts, pick, preferred_element_type=F32)
        row = both[0:1, :] * 16.0 + both[1:2, :]
        row = jnp.where(lane < counts[p], jnp.broadcast_to(row, (8, CAP)), 0.0)
        sg[p, CAP : CAP + 8, :] = row

    for i in range(2, 6):
        x_copies[i].wait_recv()
    s1[half_a, :] = rc[0, half_a, :] + (rx[3] + rx[4])
    s1[half_b, :] = rc[0, half_b, :] + (rx[2] + rx[5])

    def rows_y(k):
        return pl.ds(pl.multiple_of(k * R2, 8), R2)

    y_copies = [copy(s1.at[rows_y((y + d) % NY)], ry.at[d - 1], to_y(d)) for d in order_y]

    for cp in y_copies:
        cp.wait_recv()
    s2 = s1[rows_y(y), :]
    for d in range(1, NY):
        s2 = s2 + ry[d - 1]
    for k in range(NZ):
        s2z[k] = s2[k * R3 : (k + 1) * R3, :]

    z_copies = [copy(s2z.at[(z + d) % NZ], rz.at[d - 1], to_z(d)) for d in order_z]
    a_copies = [copy(sg.at[(y + d) % NY], ra.at[d], to_y(d)) for d in order_y]
    ra[0] = sg[y]
    for cp in z_copies:
        cp.wait_recv()
    s3 = s2z[z]
    for d in range(1, NZ):
        s3 = s3 + rz[d - 1]
    gz[z] = s3
    zg_copies = [copy(gz.at[z], gz.at[z], to_z(d)) for d in order_z]

    for cp in zg_copies:
        cp.wait_recv()
    for k in range(NZ):
        t72[k * R3 : (k + 1) * R3, :] = gz[k]

    g_ref[c, x, rows_y(y), :] = t72[...]
    yg_copies = {d: copy(t72, g_ref.at[c, x, rows_y(y)], to_y(d)) for d in order_y}

    before, after, far = (x + NX - 1) % NX, (x + 1) % NX, (x + 2) % NX
    near_first = order_y[::-1]
    pieces = [y] + [(y - d + NY) % NY for d in near_first]

    def pass_on(xs, rows, target):
        return copy(g_ref.at[c, xs, rows], g_ref.at[c, xs, rows], target)

    def whole(xs):
        return copy(g_ref.at[c, xs], g_ref.at[c, xs], to_c)

    up, down, relayed = [], [], []

    def spread(n):
        for k in range(len(up), n):
            if k > 0:
                yg_copies[near_first[k - 1]].wait_recv()
            up.append(pass_on(x, rows_y(pieces[k]), to_x(1)))
            down.append(pass_on(x, rows_y(pieces[k]), to_x(3)))

    def relay(n):
        for k in range(len(relayed), n):
            if k % 2 == 0:
                up[k].wait_recv()
                relayed.append(pass_on(before, rows_y(pieces[k]), to_x(1)))
            else:
                down[k].wait_recv()
                relayed.append(pass_on(after, rows_y(pieces[k]), to_x(3)))

    spread(1)

    for cp in a_copies:
        cp.wait_recv()
    for d in range(NY):
        v = ra[d, 0:CAP, :]
        top = v.astype(BF16)
        rhs[d * CAP : (d + 1) * CAP, 0:128] = top
        rhs[d * CAP : (d + 1) * CAP, 128:256] = (v - top.astype(F32)).astype(BF16)

    @pl.loop(0, ROWS_OWN // BLK)
    def _(b):
        cols = []
        for d in range(NY):
            rel = relative(ra[d, CAP : CAP + 8, :].astype(jnp.int32), b * BLK, BLK)
            cols.append(onehot_bf16(rel[0:1, :], iota_bf))
        lhs = jnp.concatenate(cols, axis=1)
        acc = jnp.dot(lhs, rhs[0:SLOTS, :], preferred_element_type=F32)
        table_ref[pl.ds(pl.multiple_of(b * BLK, BLK), BLK), :] = acc[:, 0:128] + acc[:, 128:256]

    spread(5)
    relay(1)
    spread(7)
    relay(3)
    spread(8)
    cg_copies = [whole(x)]
    relay(8)
    for k in range(1, NY, 2):
        up[k].wait_recv()
    cg_copies.append(whole(before))
    for k in range(0, NY, 2):
        down[k].wait_recv()
    cg_copies.append(whole(after))
    for cp in relayed:
        cp.wait_recv()
    cg_copies.append(whole(far))
    for cp in cg_copies:
        cp.wait_recv()
    for cp in sends:
        cp.wait_send()


N_COPIES = NX + 6 + 3 * (NY - 1) + 2 * (NZ - 1) + 3 * NY + NX


def finish_kernel(g_ref, table_in, freq_ref, table_ref, weight_ref, bias_ref, sem):
    cps = []

    def copy(src, dst):
        cp = pltpu.make_async_copy(src, dst, sem.at[len(cps)])
        cp.start()
        cps.append(cp)

    for h in range(2):
        for k in range(NX):
            copy(g_ref.at[h, k, 0:FX], freq_ref.at[pl.ds(h * HALF + k * FX, FX)])
            copy(g_ref.at[h, k, FX : FX + WX], weight_ref.at[pl.ds(h * 128 + k * WX, WX)])
    copy(table_in, table_ref)
    bias_ref[...] = g_ref[0, 0, FX + WX : FX + WX + 1, :]
    for cp in cps:
        cp.wait()


def per_device(lookup_slot, emb_cot, slot_row, slot_count, bottom_act, bottom_cot):
    n, f = lookup_slot.shape
    ids = lookup_slot.T
    emb = jnp.transpose(emb_cot, (1, 0, 2)).reshape(f * n, EMB)
    vm = pl.BlockSpec(memory_space=pltpu.VMEM)
    hbm = pl.BlockSpec(memory_space=pltpu.HBM)
    anym = pl.BlockSpec(memory_space=pl.ANY)
    gathered, table = pl.pallas_call(
        main_kernel,
        out_shape=(pltpu.VMEM((2, NX, R1, 128), F32), pltpu.VMEM((ROWS_OWN, 128), F32)),
        in_specs=[hbm] * 6,
        out_specs=(vm, vm),
        scratch_shapes=[
            pltpu.VMEM((f, n), jnp.int32),
            pltpu.VMEM((f * n, EMB), BF16),
            pltpu.VMEM(slot_row.shape, jnp.int32),
            pltpu.SMEM(slot_count.shape, jnp.int32),
            pltpu.VMEM(bottom_act.shape, BF16),
            pltpu.VMEM(bottom_cot.shape, BF16),
            pltpu.SemaphoreType.DMA((6,)),
            pltpu.VMEM((f * n, 256), BF16),
            pltpu.VMEM((f, n), jnp.int32),
            pltpu.VMEM((2, NX, R1, 128), F32),
            pltpu.VMEM((NX, R1, 128), F32),
            pltpu.VMEM((6, R1 // 2, 128), F32),
            pltpu.VMEM((R1, 128), F32),
            pltpu.VMEM((NY - 1, R2, 128), F32),
            pltpu.VMEM((NZ, R3, 128), F32),
            pltpu.VMEM((NZ - 1, R3, 128), F32),
            pltpu.VMEM((NZ, R3, 128), F32),
            pltpu.VMEM((R2, 128), F32),
            pltpu.VMEM((256, 128), F32),
            pltpu.VMEM((NY, CAP + 8, 128), F32),
            pltpu.VMEM((NY, CAP + 8, 128), F32),
            pltpu.SemaphoreType.DMA((N_COPIES,)),
            pltpu.SemaphoreType.DMA((N_COPIES,)),
        ],
        compiler_params=pltpu.CompilerParams(
            collective_id=0, has_side_effects=True, vmem_limit_bytes=VMEM_LIMIT
        ),
    )(*(pltpu.with_memory_space_constraint(a, pltpu.HBM) for a in (ids, emb, slot_row, slot_count, bottom_act, bottom_cot)))
    freq_grad, table_grad, weight_grad, bias_row = pl.pallas_call(
        finish_kernel,
        out_shape=(
            jax.ShapeDtypeStruct((FREQ, 128), F32),
            jax.ShapeDtypeStruct((ROWS_OWN, 128), F32),
            jax.ShapeDtypeStruct((256, 128), F32),
            jax.ShapeDtypeStruct((1, 128), F32),
        ),
        in_specs=[vm, vm],
        out_specs=(anym, anym, anym, vm),
        scratch_shapes=[pltpu.SemaphoreType.DMA((4 * NX + 1,))],
        compiler_params=pltpu.CompilerParams(vmem_limit_bytes=4 * 2**20),
    )(
        pltpu.with_memory_space_constraint(gathered, pltpu.VMEM),
        pltpu.with_memory_space_constraint(table, pltpu.VMEM),
    )
    return freq_grad, table_grad, weight_grad, bias_row.reshape(128)


def solution(mesh):
    placed = (
        P(("grp", "own"), None),
        P(("grp", "own"), None, None),
        P(("grp", "own"), None),
        P(("grp", "own"), None),
        P(("grp", "own"), None),
        P(("grp", "own"), None),
    )
    return jax.shard_map(
        per_device,
        mesh=mesh,
        in_specs=placed,
        out_specs=(P(), P(("grp", "own"), None), P(), P()),
        check_vma=False,
    )
```

```python
import functools

import jax
import jax.numpy as jnp
from jax import lax
from jax.experimental import pallas as pl
from jax.experimental.pallas import tpu as pltpu
from jax.sharding import PartitionSpec as P

MESH = pl.DeviceIdType.MESH
F32 = jnp.float32
BF16 = jnp.bfloat16

NX, NY, NZ = 4, 8, 12
FREQ = 4096
EMB = 128
SLOTS = 1024
CAP = 128
ROWS_OWN = 2048
HALF = FREQ // 2
FX = HALF // NX
WX = 128 // NX
R1 = 576
R2 = R1 // NY
R3 = R2 // NZ
BLK = 256
VMEM_LIMIT = 40 * 2**20


def nearest_last(n):
    return sorted(range(1, n), key=lambda d: -min(d, n - d))


def onehot_bf16(rows_rel, iota_bf):
    return jnp.where(iota_bf == rows_rel, jnp.ones((), BF16), jnp.zeros((), BF16))


def relative(ids, base, size):
    rel = ids - base
    ok = (rel >= 0) & (rel < size)
    return jnp.where(ok, rel, -1).astype(F32).astype(BF16)


def main_kernel(
    ids_in, emb_in, slot_row_in, counts_in, act_in, cot_in,
    g_ref, table_ref,
    ids_ref, emb_ref, slot_row_ref, counts_ref, act_ref, cot_ref, isem,
    rhs, hi_s, part, rc, rx, s1, ry, s2z, rz, gz, t72, wsc, sg, ra, ssem, rsem,
):
    loads = [
        pltpu.make_async_copy(src, dst, isem.at[i])
        for i, (src, dst) in enumerate((
            (counts_in, counts_ref), (ids_in, ids_ref), (emb_in, emb_ref),
            (cot_in, cot_ref), (act_in, act_ref), (slot_row_in, slot_row_ref),
        ))
    ]
    for ld in loads:
        ld.start()

    g = lax.axis_index("grp")
    y = lax.axis_index("own")
    x = lax.div(g, 2 * NZ)
    z = lax.rem(lax.div(g, 2), NZ)
    c = lax.rem(g, 2)

    def dev(xx, yy, zz, cc):
        return (xx * (2 * NZ) + zz * 2 + cc, yy)

    def to_x(d):
        return dev(lax.rem(x + d, NX), y, z, c)

    def to_y(d):
        return dev(x, lax.rem(y + d, NY), z, c)

    def to_z(d):
        return dev(x, y, lax.rem(z + d, NZ), c)

    to_c = dev(x, y, z, 1 - c)

    used = [0]
    sends = []
    waited = [0]

    def drain(upto):
        while waited[0] < upto:
            sends[waited[0]].wait_send()
            waited[0] += 1

    def copy(src, dst, target):
        i = used[0]
        used[0] += 1
        cp = pltpu.make_async_remote_copy(
            src_ref=src, dst_ref=dst, send_sem=ssem.at[i], recv_sem=rsem.at[i],
            device_id=target, device_id_type=MESH,
        )
        cp.start()
        sends.append(cp)
        return cp

    order_x, order_y, order_z = [2, 1, 3], nearest_last(NY), nearest_last(NZ)
    barrier = pltpu.get_barrier_semaphore()
    peers = [to_c] + [to_x(d) for d in (1, 3)] + [to_y(d) for d in order_y] + [to_z(d) for d in order_z]
    for p in peers:
        pl.semaphore_signal(barrier, inc=1, device_id=p, device_id_type=MESH)

    for ld in loads:
        ld.wait()

    counts = [counts_ref[0, p] for p in range(NY)]
    ends, total = [], 0
    for p in range(NY):
        total = total + counts[p]
        ends.append(total)
    starts = [e - n for e, n in zip(ends, counts)]
    ids = ids_ref[...]
    packed = ids - FREQ
    slot = packed
    for p in range(NY - 1):
        slot = slot + jnp.where(packed >= ends[p], CAP - counts[p], 0)
    freq = ids < FREQ
    hi_s[...] = jnp.where(freq, ids & (HALF - 1), HALF + (slot & (SLOTS // 2 - 1)))
    lo = jnp.where(freq, ids >> 11, slot >> 9).astype(F32)
    nf = ids.shape[0]
    for f in range(nf):
        col = jnp.transpose(jnp.broadcast_to(lo[f : f + 1, :], (128, 128)))
        v = emb_ref[f * 128 : (f + 1) * 128, :]
        right = v * col.astype(BF16)
        rhs[f * 128 : (f + 1) * 128, 0:128] = v * (1.0 - col).astype(BF16)
        rhs[f * 128 : (f + 1) * 128, 128:256] = right

    cot = cot_ref[...]
    wsc[...] = lax.dot_general(act_ref[...], cot, (((0,), (0,)), ((), ())), preferred_element_type=F32)
    bias = jnp.sum(cot.astype(F32), axis=0, keepdims=True)

    iota_bf = lax.broadcasted_iota(jnp.int32, (BLK, 128), 0).astype(F32).astype(BF16)

    def block_sum(base):
        rel = relative(hi_s[...], base, BLK)
        lhs = jnp.concatenate([onehot_bf16(rel[f : f + 1, :], iota_bf) for f in range(nf)], axis=1)
        return jnp.dot(lhs, rhs[...], preferred_element_type=F32)

    order = order_x + [0]
    c_copies = []
    x_copies = {}
    half_a, half_b = pl.ds(0, R1 // 2), pl.ds(R1 // 2, R1 // 2)

    def after_core(k):
        o = order[k]
        c_copies[k].wait_recv()
        rc[o] = rc[o] + part[c, o]
        if o == 2:
            x_copies[0] = copy(rc.at[2, half_a], rx.at[0], to_x(1))
            x_copies[1] = copy(rc.at[2, half_b], rx.at[1], to_x(3))
        if o == 1:
            x_copies[2] = copy(rc.at[1, half_b], rx.at[2], to_x(1))
        if o == 3:
            x_copies[3] = copy(rc.at[3, half_a], rx.at[3], to_x(3))

    for k, o in enumerate(order):
        px = lax.rem(x + o, NX)

        @pl.loop(0, FX // BLK)
        def _(b, o=o, px=px):
            acc = block_sum(px * FX + b * BLK)
            at = pl.ds(pl.multiple_of(b * BLK, BLK), BLK)
            part[0, o, at, :] = acc[:, 0:128]
            part[1, o, at, :] = acc[:, 128:256]

        for h in range(2):
            part[h, o, FX : FX + WX, :] = wsc[pl.ds(pl.multiple_of(h * 128 + px * WX, WX), WX), :]
            part[h, o, FX + WX : FX + WX + 8, :] = jnp.broadcast_to(bias, (8, 128))
            part[h, o, FX + WX + 8 : R1, :] = jnp.zeros((R1 - FX - WX - 8, 128), F32)
        if k == 0:
            pl.semaphore_wait(barrier, len(peers))
        c_copies.append(copy(part.at[1 - c, o], rc.at[o], to_c))
        if k > 0:
            after_core(k - 1)
    after_core(len(order) - 1)

    @pl.loop(0, SLOTS // 2 // BLK)
    def _(b):
        acc = block_sum(HALF + b * BLK)
        for q in range(BLK // CAP):
            sg[b * (BLK // CAP) + q, 0:CAP, :] = acc[q * CAP : (q + 1) * CAP, 0:128]
            sg[NY // 2 + b * (BLK // CAP) + q, 0:CAP, :] = acc[q * CAP : (q + 1) * CAP, 128:256]

    x_copies[0].wait_recv()
    rc[1, half_a, :] = rc[1, half_a, :] + rx[0]
    x_copies[4] = copy(rc.at[1, half_a], rx.at[4], to_x(1))
    x_copies[1].wait_recv()
    rc[3, half_b, :] = rc[3, half_b, :] + rx[1]
    x_copies[5] = copy(rc.at[3, half_b], rx.at[5], to_x(3))

    sr = jnp.broadcast_to(slot_row_ref[...], (8, SLOTS))
    which = lax.broadcasted_iota(jnp.int32, (8, SLOTS), 0)
    parts = jnp.where(which == 0, sr >> 4, sr & 15).astype(F32).astype(BF16)
    diff = lax.broadcasted_iota(jnp.int32, (SLOTS, CAP), 0) - lax.broadcasted_iota(jnp.int32, (SLOTS, CAP), 1)
    lane = lax.broadcasted_iota(jnp.int32, (8, CAP), 1)
    for p in range(NY):
        pick = jnp.where(diff == starts[p], 1.0, 0.0).astype(BF16)
        both = jnp.dot(parts, pick, preferred_element_type=F32)
        row = both[0:1, :] * 16.0 + both[1:2, :]
        row = jnp.where(lane < counts[p], jnp.broadcast_to(row, (8, CAP)), 0.0)
        sg[p, CAP : CAP + 8, :] = row

    for i in range(2, 6):
        x_copies[i].wait_recv()
    s1[half_a, :] = rc[0, half_a, :] + (rx[3] + rx[4])
    s1[half_b, :] = rc[0, half_b, :] + (rx[2] + rx[5])

    def rows_y(k):
        return pl.ds(pl.multiple_of(k * R2, 8), R2)

    y_copies = [copy(s1.at[rows_y(lax.rem(y + d, NY))], ry.at[d - 1], to_y(d)) for d in order_y]

    for cp in y_copies:
        cp.wait_recv()
    s2 = s1[rows_y(y), :]
    for d in range(1, NY):
        s2 = s2 + ry[d - 1]
    for k in range(NZ):
        s2z[k] = s2[k * R3 : (k + 1) * R3, :]

    z_copies = [copy(s2z.at[lax.rem(z + d, NZ)], rz.at[d - 1], to_z(d)) for d in order_z]
    n_reduce = len(sends)
    a_copies = [copy(sg.at[lax.rem(y + d, NY)], ra.at[d], to_y(d)) for d in order_y]
    ra[0] = sg[y]
    for cp in z_copies:
        cp.wait_recv()
    s3 = s2z[z]
    for d in range(1, NZ):
        s3 = s3 + rz[d - 1]
    gz[z] = s3
    zg_copies = [copy(gz.at[z], gz.at[z], to_z(d)) for d in order_z]

    drain(n_reduce)
    for cp in zg_copies:
        cp.wait_recv()
    for k in range(NZ):
        t72[k * R3 : (k + 1) * R3, :] = gz[k]

    n_z = len(sends)
    g_ref[c, x, rows_y(y), :] = t72[...]
    yg_copies = {d: copy(t72, g_ref.at[c, x, rows_y(y)], to_y(d)) for d in order_y}

    before, after, far = lax.rem(x + NX - 1, NX), lax.rem(x + 1, NX), lax.rem(x + 2, NX)
    near_first = order_y[::-1]
    pieces = [y] + [lax.rem(y - d + NY, NY) for d in near_first]

    def pass_on(xs, rows, target):
        return copy(g_ref.at[c, xs, rows], g_ref.at[c, xs, rows], target)

    def whole(xs):
        return copy(g_ref.at[c, xs], g_ref.at[c, xs], to_c)

    up, down, relayed = [], [], []

    def spread(n):
        for k in range(len(up), n):
            if k > 0:
                yg_copies[near_first[k - 1]].wait_recv()
            up.append(pass_on(x, rows_y(pieces[k]), to_x(1)))
            down.append(pass_on(x, rows_y(pieces[k]), to_x(3)))

    def relay(n):
        for k in range(len(relayed), n):
            if k % 2 == 0:
                up[k].wait_recv()
                relayed.append(pass_on(before, rows_y(pieces[k]), to_x(1)))
            else:
                down[k].wait_recv()
                relayed.append(pass_on(after, rows_y(pieces[k]), to_x(3)))

    spread(1)

    for cp in a_copies:
        cp.wait_recv()
    for d in range(NY):
        v = ra[d, 0:CAP, :]
        top = v.astype(BF16)
        rhs[d * CAP : (d + 1) * CAP, 0:128] = top
        rhs[d * CAP : (d + 1) * CAP, 128:256] = (v - top.astype(F32)).astype(BF16)

    drain(n_z)

    def scatter(lower, upper):
        @pl.loop(lower, upper)
        def _(b):
            cols = []
            for d in range(NY):
                rel = relative(ra[d, CAP : CAP + 8, :].astype(jnp.int32), b * BLK, BLK)
                cols.append(onehot_bf16(rel[0:1, :], iota_bf))
            lhs = jnp.concatenate(cols, axis=1)
            acc = jnp.dot(lhs, rhs[0:SLOTS, :], preferred_element_type=F32)
            table_ref[pl.ds(pl.multiple_of(b * BLK, BLK), BLK), :] = acc[:, 0:128] + acc[:, 128:256]

    blocks = ROWS_OWN // BLK
    scatter(0, blocks // 2)
    spread(5)
    relay(1)
    spread(7)
    relay(3)
    spread(8)
    cg_copies = [whole(x)]
    relay(8)
    for k in range(1, NY, 2):
        up[k].wait_recv()
    cg_copies.append(whole(before))
    for k in range(0, NY, 2):
        down[k].wait_recv()
    cg_copies.append(whole(after))
    scatter(blocks // 2, blocks)
    drain(n_z + (NY - 1) + 2 * NY)
    for cp in relayed:
        cp.wait_recv()
    cg_copies.append(whole(far))
    for cp in cg_copies:
        cp.wait_recv()
    drain(len(sends))


N_COPIES = NX + 6 + 3 * (NY - 1) + 2 * (NZ - 1) + 3 * NY + NX


def finish_kernel(g_ref, table_in, freq_ref, table_ref, weight_ref, bias_ref, sem):
    cps = []

    def copy(src, dst):
        cp = pltpu.make_async_copy(src, dst, sem.at[len(cps)])
        cp.start()
        cps.append(cp)

    for h in range(2):
        copy(g_ref.at[h, :, 0:FX], freq_ref.at[h])
    copy(table_in, table_ref)
    copy(g_ref.at[:, :, FX : FX + WX], weight_ref)
    bias_ref[...] = g_ref[0, 0, FX + WX : FX + WX + 1, :]
    for cp in cps:
        cp.wait()


def per_device(lookup_slot, emb_cot, slot_row, slot_count, bottom_act, bottom_cot):
    n, f = lookup_slot.shape
    ids = lookup_slot.T
    emb = jnp.transpose(emb_cot, (1, 0, 2)).reshape(f * n, EMB)
    vm = pl.BlockSpec(memory_space=pltpu.VMEM)
    hbm = pl.BlockSpec(memory_space=pltpu.HBM)
    anym = pl.BlockSpec(memory_space=pl.ANY)
    gathered, table = pl.pallas_call(
        main_kernel,
        out_shape=(pltpu.VMEM((2, NX, R1, 128), F32), pltpu.VMEM((ROWS_OWN, 128), F32)),
        in_specs=[hbm] * 6,
        out_specs=(vm, vm),
        scratch_shapes=[
            pltpu.VMEM((f, n), jnp.int32),
            pltpu.VMEM((f * n, EMB), BF16),
            pltpu.VMEM(slot_row.shape, jnp.int32),
            pltpu.SMEM(slot_count.shape, jnp.int32),
            pltpu.VMEM(bottom_act.shape, BF16),
            pltpu.VMEM(bottom_cot.shape, BF16),
            pltpu.SemaphoreType.DMA((6,)),
            pltpu.VMEM((f * n, 256), BF16),
            pltpu.VMEM((f, n), jnp.int32),
            pltpu.VMEM((2, NX, R1, 128), F32),
            pltpu.VMEM((NX, R1, 128), F32),
            pltpu.VMEM((6, R1 // 2, 128), F32),
            pltpu.VMEM((R1, 128), F32),
            pltpu.VMEM((NY - 1, R2, 128), F32),
            pltpu.VMEM((NZ, R3, 128), F32),
            pltpu.VMEM((NZ - 1, R3, 128), F32),
            pltpu.VMEM((NZ, R3, 128), F32),
            pltpu.VMEM((R2, 128), F32),
            pltpu.VMEM((256, 128), F32),
            pltpu.VMEM((NY, CAP + 8, 128), F32),
            pltpu.VMEM((NY, CAP + 8, 128), F32),
            pltpu.SemaphoreType.DMA((N_COPIES,)),
            pltpu.SemaphoreType.DMA((N_COPIES,)),
        ],
        compiler_params=pltpu.CompilerParams(
            collective_id=0, has_side_effects=True, vmem_limit_bytes=VMEM_LIMIT
        ),
    )(*(pltpu.with_memory_space_constraint(a, pltpu.HBM) for a in (ids, emb, slot_row, slot_count, bottom_act, bottom_cot)))
    freq_grad, table_grad, weight_grad, bias_row = pl.pallas_call(
        finish_kernel,
        out_shape=(
            jax.ShapeDtypeStruct((2, NX, FX, 128), F32),
            jax.ShapeDtypeStruct((ROWS_OWN, 128), F32),
            jax.ShapeDtypeStruct((2, NX, WX, 128), F32),
            jax.ShapeDtypeStruct((1, 128), F32),
        ),
        in_specs=[vm, vm],
        out_specs=(anym, anym, anym, vm),
        scratch_shapes=[pltpu.SemaphoreType.DMA((4,))],
        compiler_params=pltpu.CompilerParams(vmem_limit_bytes=4 * 2**20),
    )(
        pltpu.with_memory_space_constraint(gathered, pltpu.VMEM),
        pltpu.with_memory_space_constraint(table, pltpu.VMEM),
    )
    return freq_grad.reshape(FREQ, 128), table_grad, weight_grad.reshape(256, 128), bias_row.reshape(128)


def solution(mesh):
    placed = (
        P(("grp", "own"), None),
        P(("grp", "own"), None, None),
        P(("grp", "own"), None),
        P(("grp", "own"), None),
        P(("grp", "own"), None),
        P(("grp", "own"), None),
    )
    return jax.shard_map(
        per_device,
        mesh=mesh,
        in_specs=placed,
        out_specs=(P(), P(("grp", "own"), None), P(), P()),
        check_vma=False,
    )
```
